768 devices in a mesh: frame: 8 (over x, core), fsdp: 24 (over z, y_lo), head: 4 (over y_hi).
Axes of the slice: x: 4, y: 8 (y_hi: 4, y_lo: 2; y = y_hi * 2 + y_lo), z: 12, core: 2. Of those that a mesh axis runs over, the one named last changes fastest.
Arguments:
- queries: bfloat16 [2048, 61440], P('frame', ('fsdp', 'head')), may hold values from -6 to 6
- noisy_keys: bfloat16 [2048, 61440], P('frame', ('fsdp', 'head')), may hold values from -6 to 6
- noisy_values: bfloat16 [2048, 61440], P('frame', ('fsdp', 'head')), may hold values from -6 to 6
- clean_keys: bfloat16 [2048, 61440], P('frame', ('fsdp', 'head')), may hold values from -10 to 10
- clean_values: bfloat16 [2048, 61440], P('frame', ('fsdp', 'head')), may hold values from -6 to 6
- gain_query: float32 [5120], replicated, may hold values from 0.5 to 2
- gain_key: float32 [5120], replicated, may hold values from 0.5 to 2
- out_grad: bfloat16 [2048, 61440], P('frame', ('fsdp', 'head')), may hold values from -6 to 6
Outputs:
- attended: bfloat16 [2048, 61440], P('frame', ('fsdp', 'head'))
- grad_queries: bfloat16 [2048, 61440], P('frame', ('fsdp', 'head'))
- grad_keys: bfloat16 [2048, 61440], P('frame', ('fsdp', 'head'))
- grad_values: bfloat16 [2048, 61440], P('frame', ('fsdp', 'head'))
- grad_gain_query: float32 [5120], replicated
- grad_gain_key: float32 [5120], replicated
The draws below stay inside these ranges and needn't reach their ends.
All inputs are finite; a program needn't handle non-finite values.
Results may differ from the reference program's by a relative error of at most 0.012.
Values may be sent and summed in bfloat16 or wider, within the bound.
No kernel may reach another device: no remote copies, remote signals or barrier semaphores. Data moves between devices by JAX's collectives and lax.ppermute only.
A program may use at most 64 MiB of HBM per device.

```python
import math
import jax
import jax.numpy as jnp
from jax import lax

D = 5120
HEADS = 40
DH = 128
FRAME_TOK = 256
FRAMES = 8
SEQ = 2048
VIDEOS = 12


def half_scales(key, salt):
    lowest = math.log(0.2)
    drawn = jax.random.uniform(jax.random.fold_in(key, salt), (SEQ, VIDEOS, 2), jnp.float32, lowest, 0.0)
    scales = jnp.exp(drawn)
    columns = jnp.arange(VIDEOS * D)
    video_of = columns % (VIDEOS * D // 2) // (D // 2)
    half_of = columns // (VIDEOS * D // 2)
    return scales[:, video_of, half_of]


def draw_queries(key, part):
    base = jnp.clip(jax.random.normal(jax.random.fold_in(key, 11), (SEQ, VIDEOS * D), jnp.float32), -6.0, 6.0)
    base = base * half_scales(key, 4411)
    return base.astype(jnp.bfloat16)


def draw_noisy_keys(key, part):
    base = jnp.clip(jax.random.normal(jax.random.fold_in(key, 13), (SEQ, VIDEOS * D), jnp.float32), -6.0, 6.0)
    base = base * half_scales(key, 4413)
    return base.astype(jnp.bfloat16)


def draw_clean_keys(key, part):
    base = jnp.clip(jax.random.normal(jax.random.fold_in(key, 12), (SEQ, VIDEOS * D), jnp.float32), -6.0, 6.0)
    return base.astype(jnp.bfloat16)


def block_levels(key, extent, shards, smallest, top_value):
    level = 1.0
    for dim, shards_of in shards:
        draws = jax.random.uniform(jax.random.fold_in(jax.random.fold_in(key, 6), dim), (shards_of,), jnp.float32, smallest / len(shards), top_value / len(shards))
        level = level * jnp.repeat(jnp.exp(draws), extent[dim] // shards_of).reshape((-1,) + (1,) * (len(extent) - 1 - dim))
    return level


def normal_values(rng, extent, width, bound, pieces=(), kind=jnp.bfloat16):
    level = block_levels(rng, extent, pieces, -0.22, 0.18) if pieces else 1.0
    values = jax.random.normal(rng, extent, jnp.float32) * width * level
    return jnp.minimum(jnp.maximum(values, -bound), bound).astype(kind)


def setup_inputs(seed: int = 0) -> dict:
    keys = jax.random.split(jax.random.key(seed), 9)
    queries = draw_queries(jax.random.fold_in(keys[8], 71), 0)
    noisy_keys = draw_noisy_keys(jax.random.fold_in(keys[8], 71), 0)
    noisy_values = normal_values(keys[2], (SEQ, VIDEOS * D), 1.0, 6.0, ((0, 8), (1, 96)))
    clean_keys = draw_clean_keys(jax.random.fold_in(keys[8], 71), 0)
    clean_values = normal_values(keys[4], (SEQ, VIDEOS * D), 1.0, 6.0, ((0, 8), (1, 96)))
    gain_query = jnp.clip(jnp.exp(jax.random.uniform(keys[5], (D,), jnp.float32, math.log(0.5), math.log(2.0))), 0.5, 2.0)
    gain_key = jnp.clip(jnp.exp(jax.random.uniform(keys[6], (D,), jnp.float32, math.log(0.5), math.log(2.0))), 0.5, 2.0)
    out_grad = normal_values(keys[7], (SEQ, VIDEOS * D), 1.0, 6.0, ((0, 8), (1, 96)))
    return {"queries": queries, "noisy_keys": noisy_keys, "noisy_values": noisy_values, "clean_keys": clean_keys, "clean_values": clean_values, "gain_query": gain_query, "gain_key": gain_key, "out_grad": out_grad}


EPSILON = 1e-06

def rounded(values_in):
    return lax.optimization_barrier(values_in.astype(jnp.bfloat16)).astype(jnp.float32)

def normalize(raw, gain):
    full = raw.astype(jnp.float32)
    rate = lax.rsqrt(lax.optimization_barrier(jnp.mean(full * full, axis=1)) + EPSILON)
    return (full, rate, (full * rate[:, None] * gain).astype(jnp.bfloat16))

def norm_grad(full, rate, gain, grad_normed):
    flat = grad_normed * gain
    inner = lax.optimization_barrier(jnp.sum(full * flat, axis=1))
    grad_raw = rate[:, None] * flat - full * (rate * rate * rate * inner / D)[:, None]
    grad_gain = lax.optimization_barrier(jnp.sum(grad_normed * full * rate[:, None], axis=0))
    return (grad_raw.astype(jnp.bfloat16), grad_gain)

def by_video(array):
    split = array.reshape(SEQ, 2, VIDEOS, D // 2)
    return jnp.transpose(split, (2, 0, 1, 3)).reshape(VIDEOS, SEQ, D)

def by_column(array):
    split = array.reshape(VIDEOS, SEQ, 2, D // 2)
    return jnp.transpose(split, (1, 2, 0, 3)).reshape(SEQ, VIDEOS * D)

def reference(queries, noisy_keys, noisy_values, clean_keys, clean_values, gain_query, gain_key, out_grad):
    scaling = 1.0 / math.sqrt(DH)
    highest = lax.Precision.HIGHEST

    def one_video(inputs):
        video_q, video_k, video_v, video_ck, video_cv, video_g = inputs
        q_full, rate_q, normed_q = normalize(video_q, gain_query)
        k_full, rate_k, normed_k = normalize(video_k, gain_key)
        outputs, grads_q, grads_k, grads_v = ([], [], [], [])
        for frame_index in range(FRAMES):
            first_row = frame_index * FRAME_TOK
            last_row = first_row + FRAME_TOK
            query_f = normed_q[first_row:last_row].astype(jnp.float32).reshape(FRAME_TOK, HEADS, DH)
            key_all = jnp.concatenate([normed_k[first_row:last_row], video_ck[:first_row]], axis=0)
            key_all = key_all.astype(jnp.float32).reshape(-1, HEADS, DH)
            value_all = jnp.concatenate([video_v[first_row:last_row], video_cv[:first_row]], axis=0)
            value_all = value_all.astype(jnp.float32).reshape(-1, HEADS, DH)
            grad_out = video_g[first_row:last_row].astype(jnp.float32).reshape(FRAME_TOK, HEADS, DH)
            scores = jnp.einsum('qhd,khd->hqk', query_f, key_all, precision=highest) * scaling
            row_max = lax.optimization_barrier(jnp.max(scores, axis=2))
            expo = jnp.exp(scores - row_max[:, :, None])
            total = lax.optimization_barrier(jnp.sum(expo, axis=2))
            summed = jnp.einsum('hqk,khd->qhd', rounded(expo), value_all, precision=highest)
            attention_f32 = summed / jnp.transpose(total)[:, :, None]
            log_total = row_max + jnp.log(total)
            soft_probs = jnp.exp(scores - log_total[:, :, None])
            delta = jnp.transpose(lax.optimization_barrier(jnp.sum(grad_out * attention_f32, axis=2)))
            grad_probs = jnp.einsum('qhd,khd->hqk', grad_out, value_all, precision=highest)
            grad_scores = rounded(soft_probs * (grad_probs - delta[:, :, None]))
            grad_qn = jnp.einsum('hqk,khd->qhd', grad_scores, key_all, precision=highest) * scaling
            grad_kn = jnp.einsum('hqk,qhd->khd', grad_scores[:, :, :FRAME_TOK], query_f, precision=highest) * scaling
            grad_vv = jnp.einsum('hqk,qhd->khd', rounded(soft_probs[:, :, :FRAME_TOK]), grad_out, precision=highest)
            outputs.append(attention_f32.reshape(FRAME_TOK, D).astype(jnp.bfloat16))
            grads_q.append(grad_qn.reshape(FRAME_TOK, D))
            grads_k.append(grad_kn.reshape(FRAME_TOK, D))
            grads_v.append(grad_vv.reshape(FRAME_TOK, D).astype(jnp.bfloat16))
        grad_q_raw, gain_q_part = norm_grad(q_full, rate_q, gain_query, jnp.concatenate(grads_q, axis=0))
        grad_k_raw, gain_k_part = norm_grad(k_full, rate_k, gain_key, jnp.concatenate(grads_k, axis=0))
        return (jnp.concatenate(outputs, axis=0), grad_q_raw, grad_k_raw, jnp.concatenate(grads_v, axis=0), gain_q_part, gain_k_part)
    stacked = tuple((by_video(member) for member in (queries, noisy_keys, noisy_values, clean_keys, clean_values, out_grad)))
    results = lax.map(one_video, stacked)
    attended, grad_queries, grad_keys, grad_values, gain_q_parts, gain_k_parts = results
    return (by_column(attended), by_column(grad_queries), by_column(grad_keys), by_column(grad_values), lax.optimization_barrier(jnp.sum(gain_q_parts, axis=0)), lax.optimization_barrier(jnp.sum(gain_k_parts, axis=0)))
```

```python
import math

import jax
import jax.numpy as jnp
from jax import lax
from jax.sharding import Mesh
from jax.sharding import PartitionSpec as P

D = 5120
DH = 128
FRAME = ("x", "core")
FSDP_HEAD = ("half", "video_z", "video_y", "head")
HALF_HEAD = ("half", "head")
FRAMES = 8
VIDEOS = 12
HEAD_PARTS = 4
COLUMN_PARTS = 2 * HEAD_PARTS


EPSILON = 1e-06
MASKED = -1e30


def side_by_side(arrays, axis, dim, along):
    widths = [a.shape[along] for a in arrays]
    both = jnp.concatenate(arrays, axis=along)
    out = lax.all_gather(both, axis, axis=dim, tiled=True)
    return tuple(jnp.split(out, [sum(widths[:k]) for k in range(1, len(widths))], axis=along))


def from_all(x, axes, devices):
    return lax.all_to_all(jnp.broadcast_to(x[None], (devices,) + x.shape), axes, 0, 0)


def project(left_side, right_side):
    return jnp.einsum("qhd,khd->hqk", left_side, right_side, preferred_element_type=jnp.float32)


def on_device(
    queries, noisy_keys, noisy_values, clean_keys, clean_values, gain_query, gain_key, out_grad
):
    length = queries.shape[0]
    width_dev = queries.shape[1]
    head_count = width_dev // DH
    scaling = 1.0 / math.sqrt(DH)
    own_frame = lax.axis_index(FRAME)
    own_start = own_frame * length
    column_start = lax.axis_index(HALF_HEAD) * width_dev
    gain_q = lax.dynamic_slice_in_dim(gain_query, column_start, width_dev)
    gain_k = lax.dynamic_slice_in_dim(gain_key, column_start, width_dev)

    q_full = queries.astype(jnp.float32)
    k_full = noisy_keys.astype(jnp.float32)
    squares = jnp.stack([jnp.sum(q_full * q_full, axis=1), jnp.sum(k_full * k_full, axis=1)])
    squares = jnp.sum(from_all(squares, HALF_HEAD, COLUMN_PARTS), axis=0)
    rate_q = lax.rsqrt(squares[0] / D + EPSILON)
    rate_k = lax.rsqrt(squares[1] / D + EPSILON)
    normed_q = (
        (q_full * rate_q[:, None] * gain_q).astype(jnp.bfloat16).reshape(length, head_count, DH)
    )
    normed_k = (
        (k_full * rate_k[:, None] * gain_k).astype(jnp.bfloat16).reshape(length, head_count, DH)
    )
    values_own = noisy_values.reshape(length, head_count, DH)
    grads_out = out_grad.reshape(length, head_count, DH)
    own_scores = project(normed_q, normed_k) * scaling
    row_max = jnp.max(own_scores, axis=2)
    expo = jnp.exp(own_scores - row_max[:, :, None])
    totals = jnp.sum(expo, axis=2)
    summed = jnp.einsum(
        "hqk,khd->hqd", expo.astype(jnp.bfloat16), values_own, preferred_element_type=jnp.float32
    )

    def split_piece(portion):
        key_piece, value_piece = portion
        row_count = key_piece.shape[0]
        return (
            key_piece.reshape(row_count, head_count, DH),
            value_piece.reshape(row_count, head_count, DH),
            row_count,
        )

    def visible_scores(key_piece, row_count):
        scores = project(normed_q, key_piece) * scaling
        frame_of = jnp.arange(row_count, dtype=jnp.int32) // length
        return jnp.where((frame_of < own_frame)[None, None, :], scores, MASKED)

    initial = (row_max, totals, summed)
    key_piece, value_piece, row_count = split_piece(
        side_by_side((clean_keys, clean_values), FRAME, 0, 1)
    )

    def attend(status):
        running, denominator, accumulated = status
        scores = visible_scores(key_piece, row_count)
        newest = jnp.maximum(running, jnp.max(scores, axis=2))
        exponent = jnp.exp(scores - newest[:, :, None])
        factor = jnp.exp(running - newest)
        added = jnp.einsum(
            "hqk,khd->hqd",
            exponent.astype(jnp.bfloat16),
            value_piece,
            preferred_element_type=jnp.float32,
        )
        return (
            newest,
            denominator * factor + jnp.sum(exponent, axis=2),
            accumulated * factor[:, :, None] + added,
        )

    running, denominator, accumulated = lax.cond(
        jnp.int32(0) < own_start, attend, lambda status: status, initial
    )
    log_total = running + jnp.log(denominator)
    output_f32 = accumulated / denominator[:, :, None]
    attended = jnp.transpose(output_f32, (1, 0, 2)).reshape(length, width_dev).astype(jnp.bfloat16)
    delta = jnp.sum(jnp.transpose(grads_out.astype(jnp.float32), (1, 0, 2)) * output_f32, axis=2)
    soft_probs = jnp.exp(own_scores - log_total[:, :, None])
    grad_probs = project(grads_out, values_own)
    grad_scores = (soft_probs * (grad_probs - delta[:, :, None])).astype(jnp.bfloat16)
    grad_qn = (
        jnp.einsum("hqk,khd->qhd", grad_scores, normed_k, preferred_element_type=jnp.float32)
        * scaling
    )
    grad_kn = (
        jnp.einsum("hqk,qhd->khd", grad_scores, normed_q, preferred_element_type=jnp.float32)
        * scaling
    )
    grad_vv = jnp.einsum(
        "hqk,qhd->khd",
        soft_probs.astype(jnp.bfloat16),
        grads_out,
        preferred_element_type=jnp.float32,
    )
    reflect_key_piece, reflect_value_piece, reflect_row_count = split_piece(
        side_by_side((clean_keys, clean_values), FRAME, 0, 1)
    )

    def attend_back(current):
        scores = visible_scores(reflect_key_piece, reflect_row_count)
        piece_probs = jnp.exp(scores - log_total[:, :, None])
        piece_grads = project(grads_out, reflect_value_piece)
        weighted = (piece_probs * (piece_grads - delta[:, :, None])).astype(jnp.bfloat16)
        return (
            current
            + jnp.einsum(
                "hqk,khd->qhd", weighted, reflect_key_piece, preferred_element_type=jnp.float32
            )
            * scaling
        )

    grad_qn = lax.cond(jnp.int32(0) < own_start, attend_back, lambda current: current, grad_qn)
    plain_q = grad_qn.reshape(length, width_dev)
    plain_k = grad_kn.reshape(length, width_dev)
    flat_q = plain_q * gain_q
    flat_k = plain_k * gain_k
    inners = jnp.stack([jnp.sum(q_full * flat_q, axis=1), jnp.sum(k_full * flat_k, axis=1)])
    part_q = jnp.sum(plain_q * q_full * rate_q[:, None], axis=0)
    part_k = jnp.sum(plain_k * k_full * rate_k[:, None], axis=0)
    piece_width = width_dev // FRAMES
    pieces = jnp.stack([part_q.reshape(FRAMES, piece_width), part_k.reshape(FRAMES, piece_width)], axis=1)
    piece = jnp.sum(lax.all_to_all(pieces, FRAME, 0, 0), axis=0)
    sent = jnp.concatenate([inners.reshape(2 * length), piece.reshape(2 * piece_width)])
    got = from_all(sent, FSDP_HEAD, 2 * VIDEOS * HEAD_PARTS).reshape(2, VIDEOS, HEAD_PARTS, sent.shape[0])
    video = lax.axis_index(("video_z", "video_y"))
    same_video = lax.dynamic_index_in_dim(got[:, :, :, : 2 * length], video, 1, keepdims=False)
    inners = jnp.sum(same_video, axis=(0, 1)).reshape(2, length)
    gains = jnp.sum(got[:, :, :, 2 * length :], axis=1)
    gains = from_all(gains.reshape(COLUMN_PARTS * 2 * piece_width), FRAME, FRAMES)
    gains = gains.reshape(FRAMES, COLUMN_PARTS, 2, piece_width).transpose(2, 1, 0, 3).reshape(2, D)
    cube_q = rate_q * rate_q * rate_q * inners[0] / D
    cube_k = rate_k * rate_k * rate_k * inners[1] / D
    grad_queries = (rate_q[:, None] * flat_q - q_full * cube_q[:, None]).astype(jnp.bfloat16)
    grad_keys = (rate_k[:, None] * flat_k - k_full * cube_k[:, None]).astype(jnp.bfloat16)
    grad_values = grad_vv.reshape(length, width_dev).astype(jnp.bfloat16)
    return (attended, grad_queries, grad_keys, grad_values, gains[0], gains[1])


def solution(mesh):
    torus = Mesh(
        mesh.devices.reshape(4, 2, 2, 6, 2, HEAD_PARTS),
        ("x", "core", "half", "video_z", "video_y", "head"),
    )
    in_specs = (
        P(FRAME, FSDP_HEAD),
        P(FRAME, FSDP_HEAD),
        P(FRAME, FSDP_HEAD),
        P(FRAME, FSDP_HEAD),
        P(FRAME, FSDP_HEAD),
        P(),
        P(),
        P(FRAME, FSDP_HEAD),
    )
    out_specs = (
        P(FRAME, FSDP_HEAD),
        P(FRAME, FSDP_HEAD),
        P(FRAME, FSDP_HEAD),
        P(FRAME, FSDP_HEAD),
        P(),
        P(),
    )
    return jax.shard_map(
        on_device, mesh=torus, in_specs=in_specs, out_specs=out_specs, check_vma=False
    )
```

```python
import functools
import math

import jax
import jax.numpy as jnp
from jax import lax
from jax.experimental import pallas as pl
from jax.experimental.pallas import tpu as pltpu
from jax.sharding import Mesh
from jax.sharding import PartitionSpec as P

D = 5120
DH = 128
FRAME = ("x", "core")
FSDP_HEAD = ("half", "video_z", "video_y", "head")
HALF_HEAD = ("half", "head")
FRAMES = 8
VIDEOS = 12
HEAD_PARTS = 4
COLUMN_PARTS = 2 * HEAD_PARTS
EPSILON = 1e-06
MASKED = -1e30
SCALING = 1.0 / math.sqrt(DH)
LOG2E = math.log2(math.e)
NT = ((1,), (1,))
NN = ((1,), (0,))
TN = ((0,), (0,))
KEY_BLOCKS = 11
BLOCKS_USED = (1, 3, 7, 11)


def from_all(x, axes, devices):
    return lax.all_to_all(jnp.broadcast_to(x[None], (devices,) + x.shape), axes, 0, 0)


def other_core(block):
    return lax.ppermute(block, "core", [(0, 1), (1, 0)])


def gather_before(block):
    rows = block.shape[0] // 2
    near = lax.ppermute(block, "x", [(0, 1), (1, 2), (2, 3)])
    far_high = lax.ppermute(block[rows:], "x", [(0, 3), (1, 0)])
    far_low = lax.ppermute(block[:rows], "x", [(0, 3)])
    sibling = lax.ppermute(block, "core", [(0, 1)])
    middle_high = lax.ppermute(far_high, "x", [(0, 3), (3, 2)])
    onward = jnp.where(lax.axis_index("x") == 3, far_low, near[:rows])
    middle_low = lax.ppermute(onward, "x", [(2, 3), (3, 2)])
    halves = [far_high, far_low, middle_high, middle_low]
    near_other = other_core(near)
    others = [other_core(half) for half in halves]
    return [sibling, near, near_other, halves[2], others[2], halves[3], others[3], halves[0], others[0], halves[1], others[1]]


def dot(a, b, dims):
    return lax.dot_general(a, b, (dims, ((), ())), preferred_element_type=jnp.float32)


NT = ((1,), (1,))
NN = ((1,), (0,))
TN = ((0,), (0,))


def column(row):
    return jnp.transpose(jnp.broadcast_to(row, (8, row.shape[1])))[:, :1]


def attention_kernel(where_ref, squares_ref, gain_q_ref, gain_k_ref, q_ref, k_ref, v_ref, do_ref, *refs):
    pairs = refs[:KEY_BLOCKS]
    att_ref, flat_q_ref, flat_k_ref, gv_ref, inner_ref, part_ref, expo_ref, sum_q_ref, sum_k_ref = refs[KEY_BLOCKS:]
    rows, width = q_ref.shape
    rates = lax.rsqrt(jnp.sum(squares_ref[...], axis=0, keepdims=True) / D + EPSILON)
    rate_q, rate_k = column(rates[:, :rows]), column(rates[:, rows:])
    own_x, own_core = where_ref[0], where_ref[1]
    sum_q_ref[...] = jnp.zeros_like(sum_q_ref)
    sum_k_ref[...] = jnp.zeros_like(sum_k_ref)

    def one_head(remote, start):
        lanes = pl.ds(pl.multiple_of(start, DH), DH)
        value_lanes = pl.ds(pl.multiple_of(start + width, DH), DH)
        gain_q, gain_k = gain_q_ref[:, lanes], gain_k_ref[:, lanes]
        q_full, k_full = q_ref[:, lanes].astype(jnp.float32), k_ref[:, lanes].astype(jnp.float32)
        normed_q = (q_full * rate_q * gain_q).astype(jnp.bfloat16)
        normed_k = (k_full * rate_k * gain_k).astype(jnp.bfloat16)
        value, do = v_ref[:, lanes], do_ref[:, lanes]
        used = BLOCKS_USED[remote]
        starts = [0]
        for b in range(used):
            starts.append(starts[-1] + (rows if b == 0 else pairs[b - 1].shape[0]))
        starts.append(starts[-1] + pairs[used - 1].shape[0])
        key_of = lambda b: normed_k if b == 0 else pairs[b - 1][:, lanes]
        value_of = lambda b: value if b == 0 else pairs[b - 1][:, value_lanes]
        held = lambda b: slice(starts[b], starts[b + 1])
        top = None
        for b in range(1 + used):
            scores = dot(key_of(b), normed_q, NT)
            if b == 1:
                scores = jnp.where(own_core == 1, scores, MASKED)
            expo_ref[held(b), :] = scores
            highest = jnp.max(scores, axis=0, keepdims=True)
            top = highest if top is None else jnp.maximum(top, highest)
        shift = top * (SCALING * LOG2E)
        total = jnp.zeros_like(top)
        out = jnp.zeros((DH, rows), jnp.float32)
        for b in range(1 + used):
            expo = jnp.exp2(expo_ref[held(b), :] * (SCALING * LOG2E) - shift)
            expo_ref[held(b), :] = expo
            total += jnp.sum(expo, axis=0, keepdims=True)
            out += dot(value_of(b), expo.astype(jnp.bfloat16), TN)
        inverse = 1.0 / total
        out = out * inverse
        att_ref[:, lanes] = jnp.transpose(out).astype(jnp.bfloat16)
        delta = jnp.sum(jnp.transpose(do.astype(jnp.float32)) * out, axis=0, keepdims=True)
        grad_q = jnp.zeros((DH, rows), jnp.float32)
        for b in range(1, 1 + used):
            grad_probs = dot(value_of(b), do, NT)
            weighted = (expo_ref[held(b), :] * (grad_probs - delta)).astype(jnp.bfloat16)
            grad_q += dot(key_of(b), weighted, TN)
        probs = expo_ref[held(0), :] * inverse
        weighted = (probs * (dot(value, do, NT) - delta)).astype(jnp.bfloat16)
        grad_q = (grad_q * inverse + dot(normed_k, weighted, TN)) * SCALING
        grad_k = dot(weighted, normed_q, NN) * SCALING
        gv_ref[:, lanes] = dot(probs.astype(jnp.bfloat16), do, NN).astype(jnp.bfloat16)
        plain_q = jnp.transpose(grad_q)
        flat_q, flat_k = plain_q * gain_q, grad_k * gain_k
        flat_q_ref[:, lanes] = flat_q
        flat_k_ref[:, lanes] = flat_k
        part_ref[0:1, lanes] = jnp.sum(plain_q * q_full * rate_q, axis=0, keepdims=True)
        part_ref[1:2, lanes] = jnp.sum(grad_k * k_full * rate_k, axis=0, keepdims=True)
        sum_q_ref[...] += q_full * flat_q
        sum_k_ref[...] += k_full * flat_k

    def run(remote):
        @pl.loop(0, width, step=DH)
        def _(start):
            one_head(remote, start)

    for remote in range(4):
        pl.when(own_x == remote)(functools.partial(run, remote))
    inner_ref[0:1, :] = jnp.sum(jnp.transpose(sum_q_ref[...]), axis=0, keepdims=True)
    inner_ref[1:2, :] = jnp.sum(jnp.transpose(sum_k_ref[...]), axis=0, keepdims=True)


def attention(where, squares, gain_q, gain_k, queries, noisy_keys, noisy_values, out_grad, pairs):
    rows, width = queries.shape
    f32 = lambda *shape: jax.ShapeDtypeStruct(shape, jnp.float32)
    low = jax.ShapeDtypeStruct((rows, width), jnp.bfloat16)
    whole = pl.BlockSpec(memory_space=pltpu.VMEM)
    return pl.pallas_call(
        attention_kernel,
        in_specs=[pl.BlockSpec(memory_space=pltpu.SMEM)] + [whole] * (7 + KEY_BLOCKS),
        out_specs=[whole] * 6,
        scratch_shapes=[
            pltpu.VMEM((FRAMES * rows, rows), jnp.float32),
            pltpu.VMEM((rows, DH), jnp.float32),
            pltpu.VMEM((rows, DH), jnp.float32),
        ],
        out_shape=[low, f32(rows, width), f32(rows, width), low, f32(2, rows), f32(2, width)],
        compiler_params=pltpu.CompilerParams(vmem_limit_bytes=40 * 1024 * 1024),
        cost_estimate=pl.CostEstimate(flops=8_000_000_000, bytes_accessed=10_000_000, transcendentals=2_600_000),
        name="attention",
    )(where, squares, gain_q, gain_k, queries, noisy_keys, noisy_values, out_grad, *pairs)


def on_device(
    queries, noisy_keys, noisy_values, clean_keys, clean_values, gain_query, gain_key, out_grad
):
    length, width_dev = queries.shape
    column_start = lax.axis_index(HALF_HEAD) * width_dev
    gain_q = lax.dynamic_slice_in_dim(gain_query, column_start, width_dev)
    gain_k = lax.dynamic_slice_in_dim(gain_key, column_start, width_dev)
    pairs = gather_before(jnp.concatenate([clean_keys, clean_values], axis=1))
    q_full = queries.astype(jnp.float32)
    k_full = noisy_keys.astype(jnp.float32)
    squares = jnp.concatenate([jnp.sum(q_full * q_full, axis=1), jnp.sum(k_full * k_full, axis=1)])
    squares = from_all(squares, HALF_HEAD, COLUMN_PARTS)
    where = jnp.stack([lax.axis_index("x"), lax.axis_index("core")]).astype(jnp.int32)
    attended, flat_q, flat_k, grad_values, inners, parts = attention(
        where, squares, gain_q[None], gain_k[None], queries, noisy_keys, noisy_values, out_grad, pairs
    )
    piece_width = width_dev // FRAMES
    pieces = parts.reshape(2, FRAMES, piece_width).transpose(1, 0, 2)
    piece = jnp.sum(lax.all_to_all(pieces, FRAME, 0, 0), axis=0)
    sent = jnp.concatenate([inners.reshape(2 * length), piece.reshape(2 * piece_width)])
    got = from_all(sent, FSDP_HEAD, 2 * VIDEOS * HEAD_PARTS).reshape(2, VIDEOS, HEAD_PARTS, sent.shape[0])
    video = lax.axis_index(("video_z", "video_y"))
    same_video = lax.dynamic_index_in_dim(got[:, :, :, : 2 * length], video, 1, keepdims=False)
    inners = jnp.sum(same_video, axis=(0, 1)).reshape(2, length)
    gains = jnp.sum(got[:, :, :, 2 * length :], axis=1)
    gains = from_all(gains.reshape(COLUMN_PARTS * 2 * piece_width), FRAME, FRAMES)
    gains = gains.reshape(FRAMES, COLUMN_PARTS, 2, piece_width).transpose(2, 1, 0, 3).reshape(2, D)
    totals = jnp.sum(squares, axis=0)
    rate_q = lax.rsqrt(totals[:length] / D + EPSILON)
    rate_k = lax.rsqrt(totals[length:] / D + EPSILON)
    cube_q = rate_q * rate_q * rate_q * inners[0] / D
    cube_k = rate_k * rate_k * rate_k * inners[1] / D
    grad_queries = (rate_q[:, None] * flat_q - q_full * cube_q[:, None]).astype(jnp.bfloat16)
    grad_keys = (rate_k[:, None] * flat_k - k_full * cube_k[:, None]).astype(jnp.bfloat16)
    return (attended, grad_queries, grad_keys, grad_values, gains[0], gains[1])


def solution(mesh):
    torus = Mesh(
        mesh.devices.reshape(4, 2, 2, 6, 2, HEAD_PARTS),
        ("x", "core", "half", "video_z", "video_y", "head"),
    )
    in_specs = (
        P(FRAME, FSDP_HEAD),
        P(FRAME, FSDP_HEAD),
        P(FRAME, FSDP_HEAD),
        P(FRAME, FSDP_HEAD),
        P(FRAME, FSDP_HEAD),
        P(),
        P(),
        P(FRAME, FSDP_HEAD),
    )
    out_specs = (
        P(FRAME, FSDP_HEAD),
        P(FRAME, FSDP_HEAD),
        P(FRAME, FSDP_HEAD),
        P(FRAME, FSDP_HEAD),
        P(),
        P(),
    )
    return jax.shard_map(
        on_device, mesh=torus, in_specs=in_specs, out_specs=out_specs, check_vma=False
    )
```

```python
import functools
import math

import jax
import jax.numpy as jnp
from jax import lax
from jax.experimental import pallas as pl
from jax.experimental.pallas import tpu as pltpu
from jax.sharding import Mesh
from jax.sharding import PartitionSpec as P

D = 5120
DH = 128
FRAME = ("x", "core")
FSDP_HEAD = ("half", "video_z", "video_y", "head")
HALF_HEAD = ("half", "head")
FRAMES = 8
VIDEOS = 12
HEAD_PARTS = 4
COLUMN_PARTS = 2 * HEAD_PARTS
EPSILON = 1e-06
MASKED = -1e30
SCALING = 1.0 / math.sqrt(DH)
LOG2E = math.log2(math.e)
NT = ((1,), (1,))
NN = ((1,), (0,))
TN = ((0,), (0,))
KEY_BLOCKS = 11
BLOCKS_USED = (1, 3, 7, 11)


def from_all(x, axes, devices):
    return lax.all_to_all(jnp.broadcast_to(x[None], (devices,) + x.shape), axes, 0, 0)


def other_core(block):
    return lax.ppermute(block, "core", [(0, 1), (1, 0)])


def gather_first(block):
    rows = block.shape[0] // 2
    near = lax.ppermute(block, "x", [(0, 1), (1, 2), (2, 3)])
    far_high = lax.ppermute(block[rows:], "x", [(0, 3), (1, 0)])
    far_low = lax.ppermute(block[:rows], "x", [(0, 3)])
    sibling = lax.ppermute(block, "core", [(0, 1)])
    return sibling, near, far_high, far_low


def gather_second(near, far_high, far_low):
    middle_high = lax.ppermute(far_high, "x", [(0, 3), (3, 2)])
    onward = jnp.where(lax.axis_index("x") == 3, far_low, near[: far_low.shape[0]])
    middle_low = lax.ppermute(onward, "x", [(2, 3), (3, 2)])
    blocks = (near, middle_high, middle_low, far_high, far_low)
    return [b for block in blocks for b in (block, other_core(block))]


def dot(a, b, dims):
    return lax.dot_general(a, b, (dims, ((), ())), preferred_element_type=jnp.float32)


NT = ((1,), (1,))
NN = ((1,), (0,))
TN = ((0,), (0,))


def column(row):
    return jnp.transpose(jnp.broadcast_to(row, (8, row.shape[1])))[:, :1]


def attention_kernel(where_ref, squares_ref, gain_q_ref, gain_k_ref, *refs):
    sources, refs = refs[: 4 + KEY_BLOCKS], refs[4 + KEY_BLOCKS :]
    att_ref, flat_q_ref, flat_k_ref, gv_ref, inner_ref, part_ref, expo_ref, sum_q_ref, sum_k_ref = refs[:9]
    local, arrived = refs[9:-1], refs[-1]
    copies = [
        pltpu.make_async_copy(source, target, arrived.at[i])
        for i, (source, target) in enumerate(zip(sources, local))
    ]
    for copy in copies:
        copy.start()
    q_ref, k_ref, v_ref, do_ref = local[:4]
    pairs = local[4:]
    rows, width = q_ref.shape
    rates = lax.rsqrt(jnp.sum(squares_ref[...], axis=0, keepdims=True) / D + EPSILON)
    rate_q, rate_k = column(rates[:, :rows]), column(rates[:, rows:])
    own_x, own_core = where_ref[0], where_ref[1]
    sum_q_ref[...] = jnp.zeros_like(sum_q_ref)
    sum_k_ref[...] = jnp.zeros_like(sum_k_ref)
    for copy in copies:
        copy.wait()

    def one_head(remote, start):
        lanes = pl.ds(pl.multiple_of(start, DH), DH)
        value_lanes = pl.ds(pl.multiple_of(start + width, DH), DH)
        gain_q, gain_k = gain_q_ref[:, lanes], gain_k_ref[:, lanes]
        q_full, k_full = q_ref[:, lanes].astype(jnp.float32), k_ref[:, lanes].astype(jnp.float32)
        normed_q = (q_full * rate_q * gain_q).astype(jnp.bfloat16)
        normed_k = (k_full * rate_k * gain_k).astype(jnp.bfloat16)
        value, do = v_ref[:, lanes], do_ref[:, lanes]
        used = BLOCKS_USED[remote]
        starts = [0]
        for b in range(used):
            starts.append(starts[-1] + (rows if b == 0 else pairs[b - 1].shape[0]))
        starts.append(starts[-1] + pairs[used - 1].shape[0])
        key_of = lambda b: normed_k if b == 0 else pairs[b - 1][:, lanes]
        value_of = lambda b: value if b == 0 else pairs[b - 1][:, value_lanes]
        held = lambda b: slice(starts[b], starts[b + 1])
        top = None
        for b in range(1 + used):
            scores = dot(key_of(b), normed_q, NT)
            if b == 1:
                scores = jnp.where(own_core == 1, scores, MASKED)
            expo_ref[held(b), :] = scores
            highest = jnp.max(scores, axis=0, keepdims=True)
            top = highest if top is None else jnp.maximum(top, highest)
        shift = top * (SCALING * LOG2E)
        total = jnp.zeros_like(top)
        out = jnp.zeros((DH, rows), jnp.float32)
        for b in range(1 + used):
            expo = jnp.exp2(expo_ref[held(b), :] * (SCALING * LOG2E) - shift)
            expo_ref[held(b), :] = expo
            total += jnp.sum(expo, axis=0, keepdims=True)
            out += dot(value_of(b), expo.astype(jnp.bfloat16), TN)
        inverse = 1.0 / total
        out = out * inverse
        att_ref[:, lanes] = jnp.transpose(out).astype(jnp.bfloat16)
        delta = jnp.sum(jnp.transpose(do.astype(jnp.float32)) * out, axis=0, keepdims=True)
        grad_q = jnp.zeros((DH, rows), jnp.float32)
        for b in range(1, 1 + used):
            grad_probs = dot(value_of(b), do, NT)
            weighted = (expo_ref[held(b), :] * (grad_probs - delta)).astype(jnp.bfloat16)
            grad_q += dot(key_of(b), weighted, TN)
        probs = expo_ref[held(0), :] * inverse
        weighted = (probs * (dot(value, do, NT) - delta)).astype(jnp.bfloat16)
        grad_q = (grad_q * inverse + dot(normed_k, weighted, TN)) * SCALING
        grad_k = dot(weighted, normed_q, NN) * SCALING
        gv_ref[:, lanes] = dot(probs.astype(jnp.bfloat16), do, NN).astype(jnp.bfloat16)
        plain_q = jnp.transpose(grad_q)
        flat_q, flat_k = plain_q * gain_q, grad_k * gain_k
        flat_q_ref[:, lanes] = flat_q
        flat_k_ref[:, lanes] = flat_k
        part_ref[0:1, lanes] = jnp.sum(plain_q * q_full * rate_q, axis=0, keepdims=True)
        part_ref[1:2, lanes] = jnp.sum(grad_k * k_full * rate_k, axis=0, keepdims=True)
        sum_q_ref[...] += q_full * flat_q
        sum_k_ref[...] += k_full * flat_k

    def run(remote):
        @pl.loop(0, width, step=DH)
        def _(start):
            one_head(remote, start)

    for remote in range(4):
        pl.when(own_x == remote)(functools.partial(run, remote))
    inner_ref[0:1, :] = jnp.sum(jnp.transpose(sum_q_ref[...]), axis=0, keepdims=True)
    inner_ref[1:2, :] = jnp.sum(jnp.transpose(sum_k_ref[...]), axis=0, keepdims=True)


def attention(where, squares, gain_q, gain_k, queries, noisy_keys, noisy_values, out_grad, pairs):
    rows, width = queries.shape
    f32 = lambda *shape: jax.ShapeDtypeStruct(shape, jnp.float32)
    low = jax.ShapeDtypeStruct((rows, width), jnp.bfloat16)
    whole = pl.BlockSpec(memory_space=pltpu.VMEM)
    fetched = [queries, noisy_keys, noisy_values, out_grad, *pairs]
    return pl.pallas_call(
        attention_kernel,
        in_specs=[pl.BlockSpec(memory_space=pltpu.SMEM)] + [whole] * 3 + [pl.BlockSpec(memory_space=pl.ANY)] * len(fetched),
        out_specs=[whole] * 6,
        scratch_shapes=[
            pltpu.VMEM((FRAMES * rows, rows), jnp.float32),
            pltpu.VMEM((rows, DH), jnp.float32),
            pltpu.VMEM((rows, DH), jnp.float32),
            *[pltpu.VMEM(x.shape, x.dtype) for x in fetched],
            pltpu.SemaphoreType.DMA((len(fetched),)),
        ],
        out_shape=[low, f32(rows, width), f32(rows, width), low, f32(2, rows), f32(2, width)],
        compiler_params=pltpu.CompilerParams(vmem_limit_bytes=56 * 1024 * 1024),
        cost_estimate=pl.CostEstimate(flops=8_000_000_000, bytes_accessed=10_000_000, transcendentals=2_600_000),
        name="attention",
    )(where, squares, gain_q, gain_k, *fetched)


def on_device(
    queries, noisy_keys, noisy_values, clean_keys, clean_values, gain_query, gain_key, out_grad
):
    length, width_dev = queries.shape
    column_start = lax.axis_index(HALF_HEAD) * width_dev
    gain_q = lax.dynamic_slice_in_dim(gain_query, column_start, width_dev)
    gain_k = lax.dynamic_slice_in_dim(gain_key, column_start, width_dev)
    first = gather_first(jnp.concatenate([clean_keys, clean_values], axis=1))
    q_full = queries.astype(jnp.float32)
    k_full = noisy_keys.astype(jnp.float32)
    squares = jnp.concatenate([jnp.sum(q_full * q_full, axis=1), jnp.sum(k_full * k_full, axis=1)])
    squares = from_all(squares, HALF_HEAD, COLUMN_PARTS)
    squares, (sibling, *received) = lax.optimization_barrier((squares, first))
    pairs = [sibling] + gather_second(*received)
    where = jnp.stack([lax.axis_index("x"), lax.axis_index("core")]).astype(jnp.int32)
    attended, flat_q, flat_k, grad_values, inners, parts = attention(
        where, squares, gain_q[None], gain_k[None], queries, noisy_keys, noisy_values, out_grad, pairs
    )
    piece_width = width_dev // FRAMES
    pieces = parts.reshape(2, FRAMES, piece_width).transpose(1, 0, 2)
    piece = jnp.sum(lax.all_to_all(pieces, FRAME, 0, 0), axis=0)
    sent = jnp.concatenate([inners.reshape(2 * length), piece.reshape(2 * piece_width)])
    got = from_all(sent, FSDP_HEAD, 2 * VIDEOS * HEAD_PARTS).reshape(2, VIDEOS, HEAD_PARTS, sent.shape[0])
    video = lax.axis_index(("video_z", "video_y"))
    same_video = lax.dynamic_index_in_dim(got[:, :, :, : 2 * length], video, 1, keepdims=False)
    inners = jnp.sum(same_video, axis=(0, 1)).reshape(2, length)
    gains = jnp.sum(got[:, :, :, 2 * length :], axis=1)
    gains = from_all(gains.reshape(COLUMN_PARTS * 2 * piece_width), FRAME, FRAMES)
    gains = gains.reshape(FRAMES, COLUMN_PARTS, 2, piece_width).transpose(2, 1, 0, 3).reshape(2, D)
    totals = jnp.sum(squares, axis=0)
    rate_q = lax.rsqrt(totals[:length] / D + EPSILON)
    rate_k = lax.rsqrt(totals[length:] / D + EPSILON)
    cube_q = rate_q * rate_q * rate_q * inners[0] / D
    cube_k = rate_k * rate_k * rate_k * inners[1] / D
    grad_queries = (rate_q[:, None] * flat_q - q_full * cube_q[:, None]).astype(jnp.bfloat16)
    grad_keys = (rate_k[:, None] * flat_k - k_full * cube_k[:, None]).astype(jnp.bfloat16)
    return (attended, grad_queries, grad_keys, grad_values, gains[0], gains[1])


def solution(mesh):
    torus = Mesh(
        mesh.devices.reshape(4, 2, 2, 6, 2, HEAD_PARTS),
        ("x", "core", "half", "video_z", "video_y", "head"),
    )
    in_specs = (
        P(FRAME, FSDP_HEAD),
        P(FRAME, FSDP_HEAD),
        P(FRAME, FSDP_HEAD),
        P(FRAME, FSDP_HEAD),
        P(FRAME, FSDP_HEAD),
        P(),
        P(),
        P(FRAME, FSDP_HEAD),
    )
    out_specs = (
        P(FRAME, FSDP_HEAD),
        P(FRAME, FSDP_HEAD),
        P(FRAME, FSDP_HEAD),
        P(FRAME, FSDP_HEAD),
        P(),
        P(),
    )
    return jax.shard_map(
        on_device, mesh=torus, in_specs=in_specs, out_specs=out_specs, check_vma=False
    )
```

```python
import functools
import math

import jax
import jax.numpy as jnp
from jax import lax
from jax.experimental import pallas as pl
from jax.experimental.pallas import tpu as pltpu
from jax.sharding import Mesh
from jax.sharding import PartitionSpec as P

D = 5120
DH = 128
FRAME = ("x", "core")
FSDP_HEAD = ("half", "video_z", "video_y", "head")
HALF_HEAD = ("half", "head")
FRAMES = 8
VIDEOS = 12
HEAD_PARTS = 4
COLUMN_PARTS = 2 * HEAD_PARTS
EPSILON = 1e-06
MASKED = -1e30
SCALING = 1.0 / math.sqrt(DH)
LOG2E = math.log2(math.e)
NT = ((1,), (1,))
NN = ((1,), (0,))
TN = ((0,), (0,))
KEY_BLOCKS = 7
BLOCKS_USED = (1, 3, 5, 7)


def from_all(x, axes, devices):
    return lax.all_to_all(jnp.broadcast_to(x[None], (devices,) + x.shape), axes, 0, 0)


def other_core(block):
    return lax.ppermute(block, "core", [(0, 1), (1, 0)])


def gather_first(block):
    near = lax.ppermute(block, "x", [(0, 1), (1, 2), (2, 3)])
    far = lax.ppermute(block, FRAME, [(0, 6), (1, 7), (3, 1)])
    sibling = lax.ppermute(block, "core", [(0, 1)])
    return sibling, near, far


def gather_second(near, far, squares):
    onward = jnp.where(lax.axis_index("x") == 2, near, far)
    middle = lax.ppermute(onward, FRAME, [(4, 6), (1, 7), (6, 4), (7, 5)])
    half_squares = lax.ppermute(squares, "half", [(0, 1), (1, 0)])
    near_other, far_other = other_core(near), other_core(far)
    middle, half_squares = lax.optimization_barrier((middle, half_squares))
    return [near, near_other, middle, other_core(middle), far, far_other], half_squares


def dot(a, b, dims):
    return lax.dot_general(a, b, (dims, ((), ())), preferred_element_type=jnp.float32)


NT = ((1,), (1,))
NN = ((1,), (0,))
TN = ((0,), (0,))


def column(row):
    return jnp.transpose(jnp.broadcast_to(row, (8, row.shape[1])))[:, :1]


def attention_kernel(where_ref, squares_ref, half_squares_ref, gain_q_ref, gain_k_ref, *refs):
    sources, refs = refs[: 4 + KEY_BLOCKS], refs[4 + KEY_BLOCKS :]
    att_ref, flat_q_ref, flat_k_ref, gv_ref, inner_ref, part_ref, expo_ref, sum_q_ref, sum_k_ref = refs[:9]
    local, arrived = refs[9:-1], refs[-1]
    copies = [
        pltpu.make_async_copy(source, target, arrived.at[i])
        for i, (source, target) in enumerate(zip(sources, local))
    ]
    for copy in copies:
        copy.start()
    q_ref, k_ref, v_ref, do_ref = local[:4]
    pairs = local[4:]
    rows, width = q_ref.shape
    rates = lax.rsqrt((squares_ref[...] + half_squares_ref[...]) / D + EPSILON)
    rate_q, rate_k = column(rates[:, :rows]), column(rates[:, rows:])
    own_x, own_core = where_ref[0], where_ref[1]
    sum_q_ref[...] = jnp.zeros_like(sum_q_ref)
    sum_k_ref[...] = jnp.zeros_like(sum_k_ref)
    for copy in copies:
        copy.wait()

    def one_head(remote, start):
        lanes = pl.ds(pl.multiple_of(start, DH), DH)
        value_lanes = pl.ds(pl.multiple_of(start + width, DH), DH)
        gain_q, gain_k = gain_q_ref[:, lanes], gain_k_ref[:, lanes]
        q_full, k_full = q_ref[:, lanes].astype(jnp.float32), k_ref[:, lanes].astype(jnp.float32)
        normed_q = (q_full * rate_q * gain_q).astype(jnp.bfloat16)
        normed_k = (k_full * rate_k * gain_k).astype(jnp.bfloat16)
        value, do = v_ref[:, lanes], do_ref[:, lanes]
        used = BLOCKS_USED[remote]
        starts = [0]
        for b in range(used):
            starts.append(starts[-1] + (rows if b == 0 else pairs[b - 1].shape[0]))
        starts.append(starts[-1] + pairs[used - 1].shape[0])
        key_of = lambda b: normed_k if b == 0 else pairs[b - 1][:, lanes]
        value_of = lambda b: value if b == 0 else pairs[b - 1][:, value_lanes]
        held = lambda b: slice(starts[b], starts[b + 1])
        top = None
        for b in range(1 + used):
            scores = dot(key_of(b), normed_q, NT)
            if b == 1:
                scores = jnp.where(own_core == 1, scores, MASKED)
            expo_ref[held(b), :] = scores
            highest = jnp.max(scores, axis=0, keepdims=True)
            top = highest if top is None else jnp.maximum(top, highest)
        shift = top * (SCALING * LOG2E)
        total = jnp.zeros_like(top)
        out = jnp.zeros((DH, rows), jnp.float32)
        for b in range(1 + used):
            expo = jnp.exp2(expo_ref[held(b), :] * (SCALING * LOG2E) - shift)
            expo_ref[held(b), :] = expo
            total += jnp.sum(expo, axis=0, keepdims=True)
            out += dot(value_of(b), expo.astype(jnp.bfloat16), TN)
        inverse = 1.0 / total
        out = out * inverse
        att_ref[:, lanes] = jnp.transpose(out).astype(jnp.bfloat16)
        delta = jnp.sum(jnp.transpose(do.astype(jnp.float32)) * out, axis=0, keepdims=True)
        grad_q = jnp.zeros((DH, rows), jnp.float32)
        for b in range(1, 1 + used):
            grad_probs = dot(value_of(b), do, NT)
            weighted = (expo_ref[held(b), :] * (grad_probs - delta)).astype(jnp.bfloat16)
            grad_q += dot(key_of(b), weighted, TN)
        probs = expo_ref[held(0), :] * inverse
        weighted = (probs * (dot(value, do, NT) - delta)).astype(jnp.bfloat16)
        grad_q = (grad_q * inverse + dot(normed_k, weighted, TN)) * SCALING
        grad_k = dot(weighted, normed_q, NN) * SCALING
        gv_ref[:, lanes] = dot(probs.astype(jnp.bfloat16), do, NN).astype(jnp.bfloat16)
        plain_q = jnp.transpose(grad_q)
        flat_q, flat_k = plain_q * gain_q, grad_k * gain_k
        flat_q_ref[:, lanes] = flat_q
        flat_k_ref[:, lanes] = flat_k
        part_ref[0:1, lanes] = jnp.sum(plain_q * q_full * rate_q, axis=0, keepdims=True)
        part_ref[1:2, lanes] = jnp.sum(grad_k * k_full * rate_k, axis=0, keepdims=True)
        sum_q_ref[...] += q_full * flat_q
        sum_k_ref[...] += k_full * flat_k

    def run(remote):
        @pl.loop(0, width, step=DH)
        def _(start):
            one_head(remote, start)

    for remote in range(4):
        pl.when(own_x == remote)(functools.partial(run, remote))
    inner_ref[0:1, :] = jnp.sum(jnp.transpose(sum_q_ref[...]), axis=0, keepdims=True)
    inner_ref[1:2, :] = jnp.sum(jnp.transpose(sum_k_ref[...]), axis=0, keepdims=True)


def attention(where, squares, gain_q, gain_k, queries, noisy_keys, noisy_values, out_grad, pairs):
    rows, width = queries.shape
    f32 = lambda *shape: jax.ShapeDtypeStruct(shape, jnp.float32)
    low = jax.ShapeDtypeStruct((rows, width), jnp.bfloat16)
    whole = pl.BlockSpec(memory_space=pltpu.VMEM)
    fetched = [queries, noisy_keys, noisy_values, out_grad, *pairs]
    return pl.pallas_call(
        attention_kernel,
        in_specs=[pl.BlockSpec(memory_space=pltpu.SMEM)] + [whole] * 4 + [pl.BlockSpec(memory_space=pl.ANY)] * len(fetched),
        out_specs=[whole] * 6,
        scratch_shapes=[
            pltpu.VMEM((FRAMES * rows, rows), jnp.float32),
            pltpu.VMEM((rows, DH), jnp.float32),
            pltpu.VMEM((rows, DH), jnp.float32),
            *[pltpu.VMEM(x.shape, x.dtype) for x in fetched],
            pltpu.SemaphoreType.DMA((len(fetched),)),
        ],
        out_shape=[low, f32(rows, width), f32(rows, width), low, f32(2, rows), f32(2, width)],
        compiler_params=pltpu.CompilerParams(vmem_limit_bytes=56 * 1024 * 1024),
        cost_estimate=pl.CostEstimate(flops=8_000_000_000, bytes_accessed=10_000_000, transcendentals=2_600_000),
        name="attention",
    )(where, *squares, gain_q, gain_k, *fetched)


def on_device(
    queries, noisy_keys, noisy_values, clean_keys, clean_values, gain_query, gain_key, out_grad
):
    length, width_dev = queries.shape
    column_start = lax.axis_index(HALF_HEAD) * width_dev
    gain_q = lax.dynamic_slice_in_dim(gain_query, column_start, width_dev)
    gain_k = lax.dynamic_slice_in_dim(gain_key, column_start, width_dev)
    first = gather_first(jnp.concatenate([clean_keys, clean_values], axis=1))
    q_full = queries.astype(jnp.float32)
    k_full = noisy_keys.astype(jnp.float32)
    squares = jnp.concatenate([jnp.sum(q_full * q_full, axis=1), jnp.sum(k_full * k_full, axis=1)])[None]
    squares = lax.psum(squares, "head")
    where = jnp.stack([lax.axis_index("x"), lax.axis_index("core")]).astype(jnp.int32)
    squares, (sibling, *received), gain_q, gain_k, where = lax.optimization_barrier(
        (squares, first, gain_q[None], gain_k[None], where)
    )
    before, half_squares = gather_second(*received, squares)
    pairs = [sibling] + before
    squares = (squares, half_squares)
    attended, flat_q, flat_k, grad_values, inners, parts = attention(
        where, squares, gain_q, gain_k, queries, noisy_keys, noisy_values, out_grad, pairs
    )
    piece_width = width_dev // FRAMES
    pieces = parts.reshape(2, FRAMES, piece_width).transpose(1, 0, 2)
    piece = jnp.sum(lax.all_to_all(pieces, FRAME, 0, 0), axis=0)
    sent = jnp.concatenate([inners.reshape(2 * length), piece.reshape(2 * piece_width)])
    got = from_all(sent, FSDP_HEAD, 2 * VIDEOS * HEAD_PARTS).reshape(2, VIDEOS, HEAD_PARTS, sent.shape[0])
    video = lax.axis_index(("video_z", "video_y"))
    same_video = lax.dynamic_index_in_dim(got[:, :, :, : 2 * length], video, 1, keepdims=False)
    inners = jnp.sum(same_video, axis=(0, 1)).reshape(2, length)
    gains = jnp.sum(got[:, :, :, 2 * length :], axis=1)
    gains = from_all(gains.reshape(COLUMN_PARTS * 2 * piece_width), FRAME, FRAMES)
    gains = gains.reshape(FRAMES, COLUMN_PARTS, 2, piece_width).transpose(2, 1, 0, 3).reshape(2, D)
    totals = squares[0][0] + squares[1][0]
    rate_q = lax.rsqrt(totals[:length] / D + EPSILON)
    rate_k = lax.rsqrt(totals[length:] / D + EPSILON)
    cube_q = rate_q * rate_q * rate_q * inners[0] / D
    cube_k = rate_k * rate_k * rate_k * inners[1] / D
    grad_queries = (rate_q[:, None] * flat_q - q_full * cube_q[:, None]).astype(jnp.bfloat16)
    grad_keys = (rate_k[:, None] * flat_k - k_full * cube_k[:, None]).astype(jnp.bfloat16)
    return (attended, grad_queries, grad_keys, grad_values, gains[0], gains[1])


def solution(mesh):
    torus = Mesh(
        mesh.devices.reshape(4, 2, 2, 6, 2, HEAD_PARTS),
        ("x", "core", "half", "video_z", "video_y", "head"),
    )
    in_specs = (
        P(FRAME, FSDP_HEAD),
        P(FRAME, FSDP_HEAD),
        P(FRAME, FSDP_HEAD),
        P(FRAME, FSDP_HEAD),
        P(FRAME, FSDP_HEAD),
        P(),
        P(),
        P(FRAME, FSDP_HEAD),
    )
    out_specs = (
        P(FRAME, FSDP_HEAD),
        P(FRAME, FSDP_HEAD),
        P(FRAME, FSDP_HEAD),
        P(FRAME, FSDP_HEAD),
        P(),
        P(),
    )
    return jax.shard_map(
        on_device, mesh=torus, in_specs=in_specs, out_specs=out_specs, check_vma=False
    )
```

```python
import functools
import math

import jax
import jax.numpy as jnp
from jax import lax
from jax.experimental import pallas as pl
from jax.experimental.pallas import tpu as pltpu
from jax.sharding import Mesh
from jax.sharding import PartitionSpec as P

D = 5120
DH = 128
FRAME = ("x", "core")
FSDP_HEAD = ("half", "video_z", "video_y", "head")
HALF_HEAD = ("half", "head")
FRAMES = 8
VIDEOS = 12
HEAD_PARTS = 4
COLUMN_PARTS = 2 * HEAD_PARTS
EPSILON = 1e-06
MASKED = -1e30
SCALING = 1.0 / math.sqrt(DH)
LOG2E = math.log2(math.e)
NT = ((1,), (1,))
NN = ((1,), (0,))
TN = ((0,), (0,))
KEY_BLOCKS = 7
BLOCKS_USED = (1, 3, 5, 7)


def from_all(x, axes, devices):
    return lax.all_to_all(jnp.broadcast_to(x[None], (devices,) + x.shape), axes, 0, 0)


def other_core(block):
    return lax.ppermute(block, "core", [(0, 1), (1, 0)])


def gather_first(block):
    near = lax.ppermute(block, "x", [(0, 1), (1, 2), (2, 3)])
    far = lax.ppermute(block, FRAME, [(0, 6), (1, 7), (3, 1)])
    sibling = lax.ppermute(block, "core", [(0, 1)])
    return sibling, near, far


def gather_second(near, far, squares):
    onward = jnp.where(lax.axis_index("x") == 2, near, far)
    middle = lax.ppermute(onward, FRAME, [(4, 6), (1, 7), (6, 4), (7, 5)])
    half_squares = lax.ppermute(squares, "half", [(0, 1), (1, 0)])
    near_other, far_other = other_core(near), other_core(far)
    middle, half_squares = lax.optimization_barrier((middle, half_squares))
    return [near, near_other, middle, other_core(middle), far, far_other], half_squares


def dot(a, b, dims):
    return lax.dot_general(a, b, (dims, ((), ())), preferred_element_type=jnp.float32)


NT = ((1,), (1,))
NN = ((1,), (0,))
TN = ((0,), (0,))


def column(row):
    return jnp.transpose(jnp.broadcast_to(row, (8, row.shape[1])))[:, :1]


def attention_kernel(where_ref, squares_ref, half_squares_ref, gain_q_ref, gain_k_ref, *refs):
    sources, refs = refs[: 4 + KEY_BLOCKS], refs[4 + KEY_BLOCKS :]
    att_ref, flat_q_ref, flat_k_ref, gv_ref, inner_ref, part_ref, expo_ref, sum_q_ref, sum_k_ref = refs[:9]
    local, arrived = refs[9:-1], refs[-1]
    width = sources[0].shape[1]
    copies = []
    for low, high in ((0, DH), (DH, width)):
        group = []
        for source, target in zip(sources, local):
            for base in range(0, source.shape[1], width):
                lanes = slice(base + low, base + high)
                number = len(group) + sum(map(len, copies))
                group.append(pltpu.make_async_copy(source.at[:, lanes], target.at[:, lanes], arrived.at[number]))
        copies.append(group)
        for copy in group:
            copy.start()
    q_ref, k_ref, v_ref, do_ref = local[:4]
    pairs = local[4:]
    rows = q_ref.shape[0]
    rates = lax.rsqrt((squares_ref[...] + half_squares_ref[...]) / D + EPSILON)
    rate_q, rate_k = column(rates[:, :rows]), column(rates[:, rows:])
    own_x, own_core = where_ref[0] // 2, where_ref[0] % 2
    sum_q_ref[...] = jnp.zeros_like(sum_q_ref)
    sum_k_ref[...] = jnp.zeros_like(sum_k_ref)
    for copy in copies[0]:
        copy.wait()

    def one_head(remote, start):
        lanes = pl.ds(pl.multiple_of(start, DH), DH)
        value_lanes = pl.ds(pl.multiple_of(start + width, DH), DH)
        gain_q, gain_k = gain_q_ref[:, lanes], gain_k_ref[:, lanes]
        q_full, k_full = q_ref[:, lanes].astype(jnp.float32), k_ref[:, lanes].astype(jnp.float32)
        normed_q = (q_full * rate_q * gain_q).astype(jnp.bfloat16)
        normed_k = (k_full * rate_k * gain_k).astype(jnp.bfloat16)
        value, do = v_ref[:, lanes], do_ref[:, lanes]
        used = BLOCKS_USED[remote]
        starts = [0]
        for b in range(used):
            starts.append(starts[-1] + (rows if b == 0 else pairs[b - 1].shape[0]))
        starts.append(starts[-1] + pairs[used - 1].shape[0])
        key_of = lambda b: normed_k if b == 0 else pairs[b - 1][:, lanes]
        value_of = lambda b: value if b == 0 else pairs[b - 1][:, value_lanes]
        held = lambda b: slice(starts[b], starts[b + 1])
        top = None
        for b in range(1 + used):
            scores = dot(key_of(b), normed_q, NT)
            if b == 1:
                scores = jnp.where(own_core == 1, scores, MASKED)
            expo_ref[held(b), :] = scores
            highest = jnp.max(scores, axis=0, keepdims=True)
            top = highest if top is None else jnp.maximum(top, highest)
        shift = top * (SCALING * LOG2E)
        total = jnp.zeros_like(top)
        out = jnp.zeros((DH, rows), jnp.float32)
        for b in range(1 + used):
            expo = jnp.exp2(expo_ref[held(b), :] * (SCALING * LOG2E) - shift)
            expo_ref[held(b), :] = expo
            total += jnp.sum(expo, axis=0, keepdims=True)
            out += dot(value_of(b), expo.astype(jnp.bfloat16), TN)
        inverse = 1.0 / total
        out = out * inverse
        att_ref[:, lanes] = jnp.transpose(out).astype(jnp.bfloat16)
        delta = jnp.sum(jnp.transpose(do.astype(jnp.float32)) * out, axis=0, keepdims=True)
        grad_q = jnp.zeros((DH, rows), jnp.float32)
        for b in range(1, 1 + used):
            grad_probs = dot(value_of(b), do, NT)
            weighted = (expo_ref[held(b), :] * (grad_probs - delta)).astype(jnp.bfloat16)
            grad_q += dot(key_of(b), weighted, TN)
        probs = expo_ref[held(0), :] * inverse
        weighted = (probs * (dot(value, do, NT) - delta)).astype(jnp.bfloat16)
        grad_q = (grad_q * inverse + dot(normed_k, weighted, TN)) * SCALING
        grad_k = dot(weighted, normed_q, NN) * SCALING
        gv_ref[:, lanes] = dot(probs.astype(jnp.bfloat16), do, NN).astype(jnp.bfloat16)
        plain_q = jnp.transpose(grad_q)
        flat_q, flat_k = plain_q * gain_q, grad_k * gain_k
        flat_q_ref[:, lanes] = flat_q
        flat_k_ref[:, lanes] = flat_k
        part_ref[0:1, lanes] = jnp.sum(plain_q * q_full * rate_q, axis=0, keepdims=True)
        part_ref[1:2, lanes] = jnp.sum(grad_k * k_full * rate_k, axis=0, keepdims=True)
        sum_q_ref[...] += q_full * flat_q
        sum_k_ref[...] += k_full * flat_k

    @pl.loop(0, width, step=DH)
    def _(start):
        @pl.when(start == DH)
        def _():
            for copy in copies[1]:
                copy.wait()

        for remote in range(len(BLOCKS_USED)):
            pl.when(own_x == remote)(functools.partial(one_head, remote, start))

    inner_ref[0:1, :] = jnp.sum(jnp.transpose(sum_q_ref[...]), axis=0, keepdims=True)
    inner_ref[1:2, :] = jnp.sum(jnp.transpose(sum_k_ref[...]), axis=0, keepdims=True)


def attention(where, squares, gain_q, gain_k, queries, noisy_keys, noisy_values, out_grad, pairs):
    rows, width = queries.shape
    f32 = lambda *shape: jax.ShapeDtypeStruct(shape, jnp.float32)
    low = jax.ShapeDtypeStruct((rows, width), jnp.bfloat16)
    whole = pl.BlockSpec(memory_space=pltpu.VMEM)
    fetched = [queries, noisy_keys, noisy_values, out_grad, *pairs]
    return pl.pallas_call(
        attention_kernel,
        in_specs=[pl.BlockSpec(memory_space=pltpu.SMEM)] + [whole] * 4 + [pl.BlockSpec(memory_space=pl.ANY)] * len(fetched),
        out_specs=[whole] * 6,
        scratch_shapes=[
            pltpu.VMEM((FRAMES * rows, rows), jnp.float32),
            pltpu.VMEM((rows, DH), jnp.float32),
            pltpu.VMEM((rows, DH), jnp.float32),
            *[pltpu.VMEM(x.shape, x.dtype) for x in fetched],
            pltpu.SemaphoreType.DMA((2 * (4 + 2 * KEY_BLOCKS),)),
        ],
        out_shape=[low, f32(rows, width), f32(rows, width), low, f32(2, rows), f32(2, width)],
        compiler_params=pltpu.CompilerParams(vmem_limit_bytes=56 * 1024 * 1024),
        cost_estimate=pl.CostEstimate(flops=8_000_000_000, bytes_accessed=10_000_000, transcendentals=2_600_000),
        name="attention",
    )(where, *squares, gain_q, gain_k, *fetched)


def on_device(
    queries, noisy_keys, noisy_values, clean_keys, clean_values, gain_query, gain_key, out_grad
):
    length, width_dev = queries.shape
    column_start = lax.axis_index(HALF_HEAD) * width_dev
    gain_q = lax.dynamic_slice_in_dim(gain_query, column_start, width_dev)
    gain_k = lax.dynamic_slice_in_dim(gain_key, column_start, width_dev)
    first = gather_first(jnp.concatenate([clean_keys, clean_values], axis=1))
    q_full = queries.astype(jnp.float32)
    k_full = noisy_keys.astype(jnp.float32)
    squares = jnp.concatenate([jnp.sum(q_full * q_full, axis=1), jnp.sum(k_full * k_full, axis=1)])[None]
    squares = lax.psum(squares, "head")
    where = lax.axis_index(FRAME).astype(jnp.int32).reshape(1)
    squares, (sibling, *received), gain_q, gain_k, where = lax.optimization_barrier(
        (squares, first, gain_q[None], gain_k[None], where)
    )
    before, half_squares = gather_second(*received, squares)
    pairs = [sibling] + before
    squares = (squares, half_squares)
    attended, flat_q, flat_k, grad_values, inners, parts = attention(
        where, squares, gain_q, gain_k, queries, noisy_keys, noisy_values, out_grad, pairs
    )
    piece_width = width_dev // FRAMES
    pieces = parts.reshape(FRAMES, 2 * piece_width)
    piece = jnp.sum(lax.all_to_all(pieces, FRAME, 0, 0), axis=0)
    sent = jnp.concatenate([inners.reshape(2 * length), piece.reshape(2 * piece_width)])
    got = from_all(sent, FSDP_HEAD, 2 * VIDEOS * HEAD_PARTS).reshape(2, VIDEOS, HEAD_PARTS, sent.shape[0])
    video = lax.axis_index(("video_z", "video_y"))
    same_video = lax.dynamic_index_in_dim(got[:, :, :, : 2 * length], video, 1, keepdims=False)
    inners = jnp.sum(same_video, axis=(0, 1)).reshape(2, length)
    gains = jnp.sum(got[:, :, :, 2 * length :], axis=1)
    gains = from_all(gains.reshape(COLUMN_PARTS * 2 * piece_width), FRAME, FRAMES)
    gains = gains.reshape(2, FRAMES // 2, COLUMN_PARTS, 2 * piece_width).transpose(0, 2, 1, 3).reshape(2, D)
    totals = squares[0][0] + squares[1][0]
    rate_q = lax.rsqrt(totals[:length] / D + EPSILON)
    rate_k = lax.rsqrt(totals[length:] / D + EPSILON)
    cube_q = rate_q * rate_q * rate_q * inners[0] / D
    cube_k = rate_k * rate_k * rate_k * inners[1] / D
    grad_queries = (rate_q[:, None] * flat_q - q_full * cube_q[:, None]).astype(jnp.bfloat16)
    grad_keys = (rate_k[:, None] * flat_k - k_full * cube_k[:, None]).astype(jnp.bfloat16)
    return (attended, grad_queries, grad_keys, grad_values, gains[0], gains[1])


def solution(mesh):
    torus = Mesh(
        mesh.devices.reshape(4, 2, 2, 6, 2, HEAD_PARTS),
        ("x", "core", "half", "video_z", "video_y", "head"),
    )
    in_specs = (
        P(FRAME, FSDP_HEAD),
        P(FRAME, FSDP_HEAD),
        P(FRAME, FSDP_HEAD),
        P(FRAME, FSDP_HEAD),
        P(FRAME, FSDP_HEAD),
        P(),
        P(),
        P(FRAME, FSDP_HEAD),
    )
    out_specs = (
        P(FRAME, FSDP_HEAD),
        P(FRAME, FSDP_HEAD),
        P(FRAME, FSDP_HEAD),
        P(FRAME, FSDP_HEAD),
        P(),
        P(),
    )
    return jax.shard_map(
        on_device, mesh=torus, in_specs=in_specs, out_specs=out_specs, check_vma=False
    )
```

```python
import functools
import math

import jax
import jax.numpy as jnp
from jax import lax
from jax.experimental import pallas as pl
from jax.experimental.pallas import tpu as pltpu
from jax.sharding import Mesh
from jax.sharding import PartitionSpec as P

D = 5120
DH = 128
FRAME = ("x", "core")
FSDP_HEAD = ("half", "video_z", "video_y", "head")
HALF_HEAD = ("half", "head")
FRAMES = 8
VIDEOS = 12
HEAD_PARTS = 4
COLUMN_PARTS = 2 * HEAD_PARTS
EPSILON = 1e-06
MASKED = -1e30
SCALING = 1.0 / math.sqrt(DH)
LOG2E = math.log2(math.e)
NT = ((1,), (1,))
NN = ((1,), (0,))
TN = ((0,), (0,))
KEY_BLOCKS = 7
BLOCKS_USED = (1, 3, 5, 7)


def from_all(x, axes, devices):
    return lax.all_to_all(jnp.broadcast_to(x[None], (devices,) + x.shape), axes, 0, 0)


def other_core(block):
    return lax.ppermute(block, "core", [(0, 1), (1, 0)])


def gather_first(block):
    near = lax.ppermute(block, "x", [(0, 1), (1, 2), (2, 3)])
    far = lax.ppermute(block, FRAME, [(0, 6), (1, 7), (3, 1)])
    sibling = lax.ppermute(block, "core", [(0, 1)])
    return sibling, near, far


def gather_second(near, far, squares):
    onward = jnp.where(lax.axis_index("x") == 2, near, far)
    middle = lax.ppermute(onward, FRAME, [(4, 6), (1, 7), (6, 4), (7, 5)])
    half_squares = lax.ppermute(squares, "half", [(0, 1), (1, 0)])
    near_other, far_other = other_core(near), other_core(far)
    middle, half_squares = lax.optimization_barrier((middle, half_squares))
    return [near, near_other, middle, other_core(middle), far, far_other], half_squares


def dot(a, b, dims):
    return lax.dot_general(a, b, (dims, ((), ())), preferred_element_type=jnp.float32)


NT = ((1,), (1,))
NN = ((1,), (0,))
TN = ((0,), (0,))


def column(row):
    return jnp.transpose(jnp.broadcast_to(row, (8, row.shape[1])))[:, :1]


def attention_kernel(where_ref, part_of_ref, squares_ref, half_squares_ref, gain_q_ref, gain_k_ref, *refs):
    sources, refs = refs[: 4 + KEY_BLOCKS], refs[4 + KEY_BLOCKS :]
    att_ref, flat_q_ref, flat_k_ref, gv_ref, inner_ref, part_ref, expo_ref, sum_q_ref, sum_k_ref = refs[:9]
    local, arrived = refs[9:-1], refs[-1]
    width = sources[0].shape[1]
    copies = []
    for low, high in ((0, DH), (DH, width)):
        group = []
        for source, target in zip(sources, local):
            for base in range(0, source.shape[1], width):
                lanes = slice(base + low, base + high)
                number = len(group) + sum(map(len, copies))
                group.append(pltpu.make_async_copy(source.at[:, lanes], target.at[:, lanes], arrived.at[number]))
        copies.append(group)
        for copy in group:
            copy.start()
    q_ref, k_ref, v_ref, do_ref = local[:4]
    pairs = local[4:]
    rows = q_ref.shape[0]
    rates = lax.rsqrt((squares_ref[...] + half_squares_ref[...]) / D + EPSILON)
    rate_q, rate_k = column(rates[:, :rows]), column(rates[:, rows:])
    own_x, own_core = where_ref[0] // 2, where_ref[0] % 2
    sum_q_ref[...] = jnp.zeros_like(sum_q_ref)
    sum_k_ref[...] = jnp.zeros_like(sum_k_ref)
    for copy in copies[0]:
        copy.wait()

    def one_head(remote, start):
        lanes = pl.ds(pl.multiple_of(start, DH), DH)
        value_lanes = pl.ds(pl.multiple_of(start + width, DH), DH)
        gain_lanes = pl.ds(pl.multiple_of(part_of_ref[0] * width + start, DH), DH)
        gain_q, gain_k = gain_q_ref[:, gain_lanes], gain_k_ref[:, gain_lanes]
        q_full, k_full = q_ref[:, lanes].astype(jnp.float32), k_ref[:, lanes].astype(jnp.float32)
        normed_q = (q_full * rate_q * gain_q).astype(jnp.bfloat16)
        normed_k = (k_full * rate_k * gain_k).astype(jnp.bfloat16)
        value, do = v_ref[:, lanes], do_ref[:, lanes]
        used = BLOCKS_USED[remote]
        starts = [0]
        for b in range(used):
            starts.append(starts[-1] + (rows if b == 0 else pairs[b - 1].shape[0]))
        starts.append(starts[-1] + pairs[used - 1].shape[0])
        key_of = lambda b: normed_k if b == 0 else pairs[b - 1][:, lanes]
        value_of = lambda b: value if b == 0 else pairs[b - 1][:, value_lanes]
        held = lambda b: slice(starts[b], starts[b + 1])
        top = None
        for b in range(1 + used):
            scores = dot(key_of(b), normed_q, NT)
            if b == 1:
                scores = jnp.where(own_core == 1, scores, MASKED)
            expo_ref[held(b), :] = scores
            highest = jnp.max(scores, axis=0, keepdims=True)
            top = highest if top is None else jnp.maximum(top, highest)
        shift = top * (SCALING * LOG2E)
        total = jnp.zeros_like(top)
        out = jnp.zeros((DH, rows), jnp.float32)
        for b in range(1 + used):
            expo = jnp.exp2(expo_ref[held(b), :] * (SCALING * LOG2E) - shift)
            expo_ref[held(b), :] = expo
            total += jnp.sum(expo, axis=0, keepdims=True)
            out += dot(value_of(b), expo.astype(jnp.bfloat16), TN)
        inverse = 1.0 / total
        out = out * inverse
        att_ref[:, lanes] = jnp.transpose(out).astype(jnp.bfloat16)
        delta = jnp.sum(jnp.transpose(do.astype(jnp.float32)) * out, axis=0, keepdims=True)
        grad_q = jnp.zeros((DH, rows), jnp.float32)
        for b in range(1, 1 + used):
            grad_probs = dot(value_of(b), do, NT)
            weighted = (expo_ref[held(b), :] * (grad_probs - delta)).astype(jnp.bfloat16)
            grad_q += dot(key_of(b), weighted, TN)
        probs = expo_ref[held(0), :] * inverse
        weighted = (probs * (dot(value, do, NT) - delta)).astype(jnp.bfloat16)
        grad_q = (grad_q * inverse + dot(normed_k, weighted, TN)) * SCALING
        grad_k = dot(weighted, normed_q, NN) * SCALING
        gv_ref[:, lanes] = dot(probs.astype(jnp.bfloat16), do, NN).astype(jnp.bfloat16)
        plain_q = jnp.transpose(grad_q)
        flat_q, flat_k = plain_q * gain_q, grad_k * gain_k
        flat_q_ref[:, lanes] = flat_q
        flat_k_ref[:, lanes] = flat_k
        part_ref[0:1, lanes] = jnp.sum(plain_q * q_full * rate_q, axis=0, keepdims=True)
        part_ref[1:2, lanes] = jnp.sum(grad_k * k_full * rate_k, axis=0, keepdims=True)
        sum_q_ref[...] += q_full * flat_q
        sum_k_ref[...] += k_full * flat_k

    @pl.loop(0, width, step=DH)
    def _(start):
        @pl.when(start == DH)
        def _():
            for copy in copies[1]:
                copy.wait()

        for remote in range(len(BLOCKS_USED)):
            pl.when(own_x == remote)(functools.partial(one_head, remote, start))

    inner_ref[0:1, :] = jnp.sum(jnp.transpose(sum_q_ref[...]), axis=0, keepdims=True)
    inner_ref[1:2, :] = jnp.sum(jnp.transpose(sum_k_ref[...]), axis=0, keepdims=True)


def attention(where, part_of, squares, gain_q, gain_k, queries, noisy_keys, noisy_values, out_grad, pairs):
    rows, width = queries.shape
    f32 = lambda *shape: jax.ShapeDtypeStruct(shape, jnp.float32)
    low = jax.ShapeDtypeStruct((rows, width), jnp.bfloat16)
    whole = pl.BlockSpec(memory_space=pltpu.VMEM)
    fetched = [queries, noisy_keys, noisy_values, out_grad, *pairs]
    return pl.pallas_call(
        attention_kernel,
        in_specs=[pl.BlockSpec(memory_space=pltpu.SMEM)] * 2 + [whole] * 4 + [pl.BlockSpec(memory_space=pl.ANY)] * len(fetched),
        out_specs=[whole] * 6,
        scratch_shapes=[
            pltpu.VMEM((FRAMES * rows, rows), jnp.float32),
            pltpu.VMEM((rows, DH), jnp.float32),
            pltpu.VMEM((rows, DH), jnp.float32),
            *[pltpu.VMEM(x.shape, x.dtype) for x in fetched],
            pltpu.SemaphoreType.DMA((2 * (4 + 2 * KEY_BLOCKS),)),
        ],
        out_shape=[low, f32(rows, width), f32(rows, width), low, f32(2, rows), f32(2, width)],
        compiler_params=pltpu.CompilerParams(vmem_limit_bytes=56 * 1024 * 1024),
        cost_estimate=pl.CostEstimate(flops=8_000_000_000, bytes_accessed=10_000_000, transcendentals=2_600_000),
        name="attention",
    )(where, part_of, *squares, gain_q, gain_k, *fetched)


def on_device(
    queries, noisy_keys, noisy_values, clean_keys, clean_values, gain_query, gain_key, out_grad
):
    length, width_dev = queries.shape
    part_of = lax.axis_index(HALF_HEAD).astype(jnp.int32).reshape(1)
    first = gather_first(jnp.concatenate([clean_keys, clean_values], axis=1))
    q_full = queries.astype(jnp.float32)
    k_full = noisy_keys.astype(jnp.float32)
    squares = jnp.concatenate([jnp.sum(q_full * q_full, axis=1), jnp.sum(k_full * k_full, axis=1)])[None]
    squares = lax.psum(squares, "head")
    where = lax.axis_index(FRAME).astype(jnp.int32).reshape(1)
    squares, (sibling, *received) = lax.optimization_barrier((squares, first))
    before, half_squares = gather_second(*received, squares)
    pairs = [sibling] + before
    squares = (squares, half_squares)
    attended, flat_q, flat_k, grad_values, inners, parts = attention(
        where, part_of, squares, gain_query[None], gain_key[None], queries, noisy_keys, noisy_values, out_grad, pairs
    )
    piece_width = width_dev // FRAMES
    pieces = parts.reshape(FRAMES, 2 * piece_width)
    piece = jnp.sum(lax.all_to_all(pieces, FRAME, 0, 0), axis=0)
    sent = jnp.concatenate([inners.reshape(2 * length), piece.reshape(2 * piece_width)])
    got = from_all(sent, FSDP_HEAD, 2 * VIDEOS * HEAD_PARTS).reshape(2, VIDEOS, HEAD_PARTS, sent.shape[0])
    video = lax.axis_index(("video_z", "video_y"))
    same_video = lax.dynamic_index_in_dim(got[:, :, :, : 2 * length], video, 1, keepdims=False)
    inners = jnp.sum(same_video, axis=(0, 1)).reshape(2, length)
    gains = jnp.sum(got[:, :, :, 2 * length :], axis=1)
    gains = from_all(gains.reshape(COLUMN_PARTS * 2 * piece_width), FRAME, FRAMES)
    gains = gains.reshape(2, FRAMES // 2, COLUMN_PARTS, 2 * piece_width).transpose(0, 2, 1, 3).reshape(2, D)
    totals = squares[0][0] + squares[1][0]
    rate_q = lax.rsqrt(totals[:length] / D + EPSILON)
    rate_k = lax.rsqrt(totals[length:] / D + EPSILON)
    cube_q = rate_q * rate_q * rate_q * inners[0] / D
    cube_k = rate_k * rate_k * rate_k * inners[1] / D
    grad_queries = (rate_q[:, None] * flat_q - q_full * cube_q[:, None]).astype(jnp.bfloat16)
    grad_keys = (rate_k[:, None] * flat_k - k_full * cube_k[:, None]).astype(jnp.bfloat16)
    return (attended, grad_queries, grad_keys, grad_values, gains[0], gains[1])


def solution(mesh):
    torus = Mesh(
        mesh.devices.reshape(4, 2, 2, 6, 2, HEAD_PARTS),
        ("x", "core", "half", "video_z", "video_y", "head"),
    )
    in_specs = (
        P(FRAME, FSDP_HEAD),
        P(FRAME, FSDP_HEAD),
        P(FRAME, FSDP_HEAD),
        P(FRAME, FSDP_HEAD),
        P(FRAME, FSDP_HEAD),
        P(),
        P(),
        P(FRAME, FSDP_HEAD),
    )
    out_specs = (
        P(FRAME, FSDP_HEAD),
        P(FRAME, FSDP_HEAD),
        P(FRAME, FSDP_HEAD),
        P(FRAME, FSDP_HEAD),
        P(),
        P(),
    )
    return jax.shard_map(
        on_device, mesh=torus, in_specs=in_specs, out_specs=out_specs, check_vma=False
    )
```
